1024 devices in a mesh: gx: 8 (over z_hi, core), gy: 16 (over x, y), gz: 8 (over z_lo).
Axes of the slice: x: 4, y: 4, z: 32 (z_hi: 4, z_lo: 8; z = z_hi * 8 + z_lo), core: 2. Of those that a mesh axis runs over, the one named last changes fastest.
Arguments:
- offsets: float32 [3, 16, 32, 16, 128], P(None, 'gx', 'gy', 'gz'), may hold values from 0 to 1
- velocity: float32 [3, 16, 32, 16, 128], P(None, 'gx', 'gy', 'gz'), may hold values from -6 to 6
- mass: float32 [16, 32, 16, 128], P('gx', 'gy', 'gz'), may hold values from 0.005 to 0.02
- counts: int32 [16, 32, 16], P('gx', 'gy', 'gz'), may hold values from 1 to 128
Outputs:
- accel: float32 [3, 16, 32, 16, 128], P(None, 'gx', 'gy', 'gz')
- density: float32 [16, 32, 16, 128], P('gx', 'gy', 'gz')
The draws below stay inside these ranges and needn't reach their ends.
Inputs may be any that keep to these rules, and one draw needn't show every extreme that they name: `counts`: slots of a cell at or beyond its count are empty.
All inputs are finite; a program needn't handle non-finite values.
Results may differ from the reference program's by a relative error of at most 0.0003.
Values sent between devices are 32-bit elements; how exact they have to be, the bound alone decides.
A program may use at most 64 MiB of HBM per device.

```python
import math
import jax
import jax.numpy as jnp
from jax import lax

P_SIZE = 128
NCX = 16
NCY = 32
NCZ = 16


def touch_ends(values, own_key, low, high):
    extent = values.shape
    place = [jax.random.randint(jax.random.fold_in(own_key, axis), (), 0, extent[axis]) for axis in range(len(extent))]
    values = values.at[tuple(place)].set(low)
    longest = extent.index(max(extent))
    place[longest] = (place[longest] + 1) % extent[longest]
    return values.at[tuple(place)].set(high)


def block_scale(own_key, extent, pieces, least, top_value):
    def one(dim, parts):
        heights = jax.random.uniform(jax.random.fold_in(jax.random.fold_in(own_key, 6), dim), (parts,), jnp.float32, least / len(pieces), top_value / len(pieces))
        return jnp.repeat(jnp.exp(heights), extent[dim] // parts).reshape((-1,) + (1,) * (len(extent) - dim - 1))

    factor_of = one(*pieces[0])
    for cut in pieces[1:]:
        factor_of = factor_of * one(*cut)
    return factor_of


def normal_values(key, extent, spread, most, split=(), held_as=jnp.bfloat16):
    gain = block_scale(key, extent, split, -0.22, 0.18) if split else 1.0
    values = jax.random.normal(key, extent, jnp.float32) * spread * gain
    return jnp.minimum(jnp.maximum(values, -most), most).astype(held_as)


def setup_inputs(seed: int = 0) -> dict:
    splits = jax.random.split(jax.random.key(seed), 5)
    offsets = jnp.clip(1.0 * jax.random.uniform(splits[0], (3, NCX, NCY, NCZ, P_SIZE), jnp.float32) ** block_scale(splits[0], (3, NCX, NCY, NCZ, P_SIZE), ((1, 8), (2, 16), (3, 8)), -0.2, 0.2), 0.0, 1.0)
    velocity = normal_values(splits[1], (3, NCX, NCY, NCZ, P_SIZE), 1.0, 6.0, ((1, 8), (2, 16), (3, 8)), jnp.float32)
    mass = jnp.clip(jnp.exp(math.log(0.02) - 1.3862944 * jax.random.uniform(splits[2], (NCX, NCY, NCZ, P_SIZE), jnp.float32) ** block_scale(splits[2], (NCX, NCY, NCZ, P_SIZE), ((0, 8), (1, 16), (2, 8)), -0.2, 0.2)), 0.005, 0.02)
    counts = touch_ends(jax.random.randint(splits[3], (NCX, NCY, NCZ), 1, P_SIZE + 1), jax.random.fold_in(splits[3], 1), 1, P_SIZE).astype(jnp.int32)
    return {"offsets": offsets, "velocity": velocity, "mass": mass, "counts": counts}


KERNEL_NORM = 315.0 / (64.0 * math.pi)
GRADIENT_NORM = 6.0 * KERNEL_NORM
PRESSURE_COEF = 0.5
VISCOSITY = 0.5
NEIGHBOUR_STEPS = [(a - 1, b - 1, c - 1) for a in range(3) for b in range(3) for c in range(3)]


def plane_map(plane_fn, own_cells, near_cells):
    planes = (jnp.moveaxis(own_cells, 1, 0), jnp.moveaxis(near_cells, 1, 0))
    results = lax.map(lambda items: plane_fn(items[0], items[1]), planes)
    return jnp.moveaxis(results, 0, 1)


def pair_geometry(own_pos, near_pos, offset_vec):
    displace = own_pos[..., :, None] - near_pos[..., None, :] - offset_vec[:, None, None, None, None]
    dist_sq = jnp.sum(displace * displace, axis=0)
    falloff = jnp.maximum(1.0 - dist_sq, 0.0)
    return displace, falloff


def density_plane(own_cells, near_cells, offset_vec):
    displace, falloff = pair_geometry(own_cells[0:3], near_cells[0:3], offset_vec)
    kernel = KERNEL_NORM * falloff * falloff * falloff
    return jnp.sum(near_cells[3][..., None, :] * kernel, axis=-1)[None]


def force_plane(own_cells, near_cells, offset_vec):
    displace, falloff = pair_geometry(own_cells[0:3], near_cells[0:3], offset_vec)
    kernel = KERNEL_NORM * falloff * falloff * falloff
    gradient = GRADIENT_NORM * falloff * falloff
    near_mass = near_cells[3][..., None, :]
    near_rho = jnp.where(near_mass > 0.0, near_cells[7][..., None, :], 1.0)
    near_press = PRESSURE_COEF / near_rho
    pair_coef = near_mass * (own_cells[6][..., :, None] + near_press) * gradient
    viscous = VISCOSITY * near_mass / near_rho * kernel
    pressure_part = jnp.sum(pair_coef[None] * displace, axis=-1)
    velocity_gap = near_cells[4:7][..., None, :] - own_cells[3:6][..., :, None]
    return pressure_part + jnp.sum(viscous[None] * velocity_gap, axis=-1)


def cell_slice(padded, step_x, step_y, step_z, size_x, size_y, size_z):
    return padded[:, 1 + step_x:1 + step_x + size_x, 1 + step_y:1 + step_y + size_y, 1 + step_z:1 + step_z + size_z]


def accumulate(plane_fn, own_cells, padded):
    size_x, size_y, size_z = own_cells.shape[1], own_cells.shape[2], own_cells.shape[3]
    running = None
    for step_x, step_y, step_z in NEIGHBOUR_STEPS:
        offset_vec = jnp.array([step_x, step_y, step_z], jnp.float32)
        near_cells = cell_slice(padded, step_x, step_y, step_z, size_x, size_y, size_z)
        contribution = plane_map(lambda own, near: plane_fn(own, near, offset_vec), own_cells, near_cells)
        running = contribution if running is None else running + contribution
    return running


def pad_cycle(field):
    return jnp.pad(field, ((0, 0), (1, 1), (1, 1), (1, 1), (0, 0)))


def reference(offsets, velocity, mass, counts):
    slot_index = lax.broadcasted_iota(jnp.int32, counts.shape + (P_SIZE,), 3)
    occupied = (slot_index < counts[..., None]).astype(jnp.float32)
    mass_eff = mass * occupied
    rim_state = pad_cycle(jnp.concatenate([offsets, mass_eff[None]], axis=0))
    density_raw = accumulate(density_plane, offsets, rim_state)
    density = density_raw * occupied[None]
    flow_state = pad_cycle(jnp.concatenate([velocity, density], axis=0))
    near_state = jnp.concatenate([rim_state, flow_state], axis=0)
    rho_safe = jnp.where(occupied[None] > 0.0, density, 1.0)
    own_state = jnp.concatenate([offsets, velocity, PRESSURE_COEF / rho_safe], axis=0)
    accel = accumulate(force_plane, own_state, near_state) * occupied[None]
    return accel, density[0]
```

```python
import functools
import math

import jax
import jax.numpy as jnp
from jax import lax
from jax.experimental import pallas as pl
from jax.experimental.pallas import tpu as pltpu
from jax.sharding import PartitionSpec as P

KERNEL_NORM = 315.0 / (64.0 * math.pi)
GRADIENT_RATIO = 6.0
PRESSURE_COEF = 0.5
AXES = ("gx", "gy", "gz")
SIDES = (-1, 0, 1)
MESH = pl.DeviceIdType.MESH
F32 = jnp.float32
TILE = 32


def span_own(step):
    if isinstance(step, int):
        return pl.ds(0, 2) if step == 0 else pl.ds((step + 1) // 2, 1)
    return pl.ds((step + 1) // 2, 1)


def span_halo(step):
    if isinstance(step, int):
        return pl.ds(1, 2) if step == 0 else pl.ds(0 if step < 0 else 3, 1)
    return pl.ds(3 * ((step + 1) // 2), 1)


def slot(step):
    return (step[0] + 1) * 9 + (step[1] + 1) * 3 + (step[2] + 1)


def kernel(sizes, off, vel, mass, cnt, acc_out, den_out, own, near, u_own, u_near, own_b, s_b, dens, force, quad,
           send1, recv1, send2, recv2):
    me = tuple(lax.axis_index(a) for a in AXES)
    near_x = 1 - 2 * lax.rem(me[0], 2)
    far_x = -near_x
    plane_dirs = [(0, b, c) for b in SIDES for c in SIDES if (b, c) != (0, 0)]
    near_dirs = [(near_x, b, c) for b in SIDES for c in SIDES]
    far_dirs = [(far_x, b, c) for b in SIDES for c in SIDES]
    all_dirs = far_dirs + near_dirs + plane_dirs

    def other(step):
        return tuple(m + s for m, s in zip(me, step))

    def exists(step):
        ok = None
        for m, s, n in zip(me, step, sizes):
            if isinstance(s, int) and s == 0:
                continue
            here = jnp.logical_and(m + s >= 0, m + s < n)
            ok = here if ok is None else jnp.logical_and(ok, here)
        return ok

    def neg(step):
        return tuple(-s for s in step)

    barrier = pltpu.get_barrier_semaphore()
    for step in all_dirs:
        @pl.when(exists(step))
        def _():
            pl.semaphore_signal(barrier, inc=1, device_id=other(step), device_id_type=MESH)

    lanes = lax.broadcasted_iota(jnp.int32, (1, 128), 1)
    for x in range(2):
        for y in range(2):
            for z in range(2):
                pos = [off[k, x, y, z : z + 1, :] + float(c - 1) for k, c in enumerate((x, y, z))]
                m_eff = jnp.where(lanes < cnt[x, y, z], mass[x, y, z : z + 1, :], 0.0)
                sq = pos[0] * pos[0] + pos[1] * pos[1] + pos[2] * pos[2]
                v = [vel[k, x, y, z : z + 1, :] for k in range(3)]
                tile = jnp.concatenate(pos + [m_eff] + v + [sq], axis=0)
                own[x, y, z] = tile
                scaled = jnp.concatenate([p * -6.0 for p in pos] + [m_eff] + v + [1.0 - sq], axis=0)
                near[1 + x, 1 + y, 1 + z] = scaled

    peers = 1
    for m, n in zip(me, sizes):
        peers = peers * (1 + (m > 0).astype(jnp.int32) + (m < n - 1).astype(jnp.int32))
    pl.semaphore_wait(barrier, peers - 1)

    def copy1(step, incoming):
        there = step if incoming else neg(step)
        return pltpu.make_async_remote_copy(
            src_ref=own.at[tuple(span_own(s) for s in step)],
            dst_ref=near.at[tuple(span_halo(s) for s in there)],
            send_sem=send1.at[slot(step)],
            recv_sem=recv1.at[slot(there)],
            device_id=other(step),
            device_id_type=MESH,
        )

    def copy2(step, incoming):
        there = step if incoming else neg(step)
        return pltpu.make_async_remote_copy(
            src_ref=u_own.at[tuple(span_own(s) for s in step)],
            dst_ref=u_near.at[tuple(span_halo(s) for s in there)],
            send_sem=send2.at[slot(step)],
            recv_sem=recv2.at[slot(there)],
            device_id=other(step),
            device_id_type=MESH,
        )

    for step in all_dirs:
        @pl.when(exists(step))
        def _():
            copy1(step, False).start()

    for n in range(8):
        x, y, z = n // 4, (n // 2) % 2, n % 2
        turned = jnp.transpose(own[x, y, z], (1, 0))
        for k in range(3):
            own_b[k, n] = jnp.broadcast_to(turned[:, k : k + 1] * (-1.0 / 3.0), (128, 128))
        own_b[3, n] = jnp.broadcast_to(turned[:, 7:8], (128, 128))

    def cells_own(x, y, z):
        return [(a, b, c) for a in (1, 2) for b in (1, 2) for c in (1, 2)]

    def cells_plane(x, y, z):
        bh, ch = 3 * y, 3 * z
        ring = [(bh, ch), (bh, 1), (bh, 2), (1, ch), (2, ch)]
        return [(a, b, c) for a in (1, 2) for b, c in ring]

    def cells_side(x, y, z):
        return [(3 * x, y + b, z + c) for b in range(3) for c in range(3)]

    def density_tile(n, r0, cells, base, first):
        rows = pl.ds(r0, TILE)
        xi, yi, zi, wi = (own_b[k, n, rows, :] for k in range(4))
        total = jnp.zeros((TILE, 128), F32) if first else dens[n, rows, :]
        for k, (a, b, c) in enumerate(cells):
            t = near[a, b, c]
            q = jnp.maximum(xi * t[0:1] + yi * t[1:2] + zi * t[2:3] + (t[7:8] - wi), 0.0)
            quad[n, base + k, rows, :] = q
            total = total + (q * q) * (q * t[3:4])
        dens[n, rows, :] = total

    def force_tile(n, r0, cells, base, first):
        rows = pl.ds(r0, TILE)
        si = s_b[n, rows, :]
        sums = [jnp.zeros((TILE, 128), F32) if first else force[k, n, rows, :] for k in range(5)]
        for k, (a, b, c) in enumerate(cells):
            t = near[a, b, c]
            q = quad[n, base + k, rows, :]
            q2 = q * q
            pr = q2 * (t[3:4] * si + t[7:8])
            vi = q2 * (q * t[7:8])
            for d in range(3):
                sums[d] = sums[d] + (pr * t[d : d + 1] + vi * t[4 + d : 5 + d])
            sums[3] = sums[3] + pr
            sums[4] = sums[4] + vi
        for k in range(5):
            force[k, n, rows, :] = sums[k]

    def sweep(tile_fn, x_side, cells_of, base, first):
        count = (8 if x_side is None else 4) * (128 // TILE)

        def step(i, carry):
            cell, r0 = i // (128 // TILE), pl.multiple_of((i % (128 // TILE)) * TILE, TILE)
            x = cell // 4 if x_side is None else x_side
            y, z = (cell // 2) % 2, cell % 2
            tile_fn(4 * x + 2 * y + z, r0, cells_of(x, y, z), base, first)
            return carry

        lax.fori_loop(0, count, step, 0)

    def arrive1(dirs):
        for step in dirs:
            region = tuple(span_halo(s) for s in step)

            @pl.when(exists(step))
            def _():
                copy1(step, True).wait_recv()
                t = near[region]
                p = []
                for k in range(3):
                    shift = 2 * step[k]
                    shift = float(shift) if isinstance(shift, int) else shift.astype(F32)
                    p.append(t[:, :, :, k : k + 1, :] + shift)
                sq = p[0] * p[0] + p[1] * p[1] + p[2] * p[2]
                for k in range(3):
                    near[region + (pl.ds(k, 1),)] = p[k] * -6.0
                near[region + (pl.ds(7, 1),)] = 1.0 - sq

            @pl.when(jnp.logical_not(exists(step)))
            def _():
                near[region] = jnp.zeros_like(near[region])

    def arrive2(dirs):
        for step in dirs:
            region = tuple(span_halo(s) for s in step)

            @pl.when(exists(step))
            def _():
                copy2(step, True).wait_recv()
                near[region + (pl.ds(7, 1),)] = u_near[region]

    near_side, far_side = (near_x + 1) // 2, (far_x + 1) // 2
    sweep(density_tile, None, cells_own, 0, True)
    arrive1(plane_dirs)
    sweep(density_tile, None, cells_plane, 8, False)
    arrive1(near_dirs)
    sweep(density_tile, near_side, cells_side, 18, False)
    arrive1(far_dirs)
    sweep(density_tile, far_side, cells_side, 18, False)

    s_rows = []
    for n in range(8):
        x, y, z = n // 4, (n // 2) % 2, n % 2
        rho = KERNEL_NORM * jnp.sum(jnp.transpose(dens[n], (1, 0)), axis=0, keepdims=True)
        held = lanes < cnt[x, y, z]
        rho = jnp.where(held, rho, 0.0)
        den_out[x, y, z : z + 1, :] = rho
        s = PRESSURE_COEF / jnp.where(held, rho, 1.0)
        s_rows.append(s)
        u = own[x, y, z, 3:4, :] * s
        u_own[x, y, z] = u
        near[1 + x, 1 + y, 1 + z, 7:8, :] = u

    for step in all_dirs:
        @pl.when(exists(step))
        def _():
            copy2(step, False).start()

    turned = jnp.transpose(jnp.concatenate(s_rows, axis=0), (1, 0))
    for n in range(8):
        s_b[n] = jnp.broadcast_to(turned[:, n : n + 1], (128, 128))

    sweep(force_tile, None, cells_own, 0, True)
    arrive2(plane_dirs)
    sweep(force_tile, None, cells_plane, 8, False)
    arrive2(near_dirs)
    sweep(force_tile, near_side, cells_side, 18, False)
    arrive2(far_dirs)
    sweep(force_tile, far_side, cells_side, 18, False)

    for n in range(8):
        x, y, z = n // 4, (n // 2) % 2, n % 2
        f = [jnp.sum(jnp.transpose(force[k, n], (1, 0)), axis=0, keepdims=True) for k in range(5)]
        held = lanes < cnt[x, y, z]
        t = own[x, y, z]
        for k in range(3):
            a = KERNEL_NORM * (f[k] + GRADIENT_RATIO * t[k : k + 1] * f[3] - t[4 + k : 5 + k] * f[4])
            acc_out[k, x, y, z : z + 1, :] = jnp.where(held, a, 0.0)

    for step in all_dirs:
        @pl.when(exists(step))
        def _():
            copy1(step, False).wait_send()
            copy2(step, False).wait_send()


def local(sizes, offsets, velocity, mass, counts):
    vmem = pl.BlockSpec(memory_space=pltpu.VMEM)
    return pl.pallas_call(
        functools.partial(kernel, sizes),
        out_shape=(
            jax.ShapeDtypeStruct(offsets.shape, F32),
            jax.ShapeDtypeStruct(mass.shape, F32),
        ),
        in_specs=[vmem, vmem, vmem, pl.BlockSpec(memory_space=pltpu.SMEM)],
        out_specs=(vmem, vmem),
        scratch_shapes=[
            pltpu.VMEM((2, 2, 2, 8, 128), F32),
            pltpu.VMEM((4, 4, 4, 8, 128), F32),
            pltpu.VMEM((2, 2, 2, 1, 128), F32),
            pltpu.VMEM((4, 4, 4, 1, 128), F32),
            pltpu.VMEM((4, 8, 128, 128), F32),
            pltpu.VMEM((8, 128, 128), F32),
            pltpu.VMEM((8, 128, 128), F32),
            pltpu.VMEM((5, 8, 128, 128), F32),
            pltpu.VMEM((8, 27, 128, 128), F32),
            pltpu.SemaphoreType.DMA((27,)),
            pltpu.SemaphoreType.DMA((27,)),
            pltpu.SemaphoreType.DMA((27,)),
            pltpu.SemaphoreType.DMA((27,)),
        ],
        compiler_params=pltpu.CompilerParams(
            collective_id=0, has_side_effects=True, vmem_limit_bytes=40 * 2**20
        ),
        name="sph",
    )(offsets, velocity, mass, counts)


def solution(mesh):
    sizes = tuple(mesh.shape[a] for a in AXES)
    in_specs = (
        P(None, "gx", "gy", "gz", None),
        P(None, "gx", "gy", "gz", None),
        P("gx", "gy", "gz", None),
        P("gx", "gy", "gz"),
    )
    out_specs = (P(None, "gx", "gy", "gz", None), P("gx", "gy", "gz", None))
    return jax.shard_map(
        functools.partial(local, sizes), mesh=mesh, in_specs=in_specs, out_specs=out_specs, check_vma=False
    )
```

```python
import functools
import math

import jax
import jax.numpy as jnp
from jax import lax
from jax.experimental import pallas as pl
from jax.experimental.pallas import tpu as pltpu
from jax.sharding import PartitionSpec as P

KERNEL_NORM = 315.0 / (64.0 * math.pi)
GRADIENT_RATIO = 6.0
PRESSURE_COEF = 0.5
AXES = ("gx", "gy", "gz")
SIDES = (-1, 0, 1)
MESH = pl.DeviceIdType.MESH
F32 = jnp.float32
BF16 = jnp.bfloat16
TILE = 32
LAST = (((1,), (1,)), ((), ()))
SHARED = (6, 4, 6)


def span_own(step):
    if isinstance(step, int):
        return pl.ds(0, 2) if step == 0 else pl.ds((step + 1) // 2, 1)
    return pl.ds((step + 1) // 2, 1)


def span_halo(step):
    if isinstance(step, int):
        return pl.ds(1, 2) if step == 0 else pl.ds(0 if step < 0 else 3, 1)
    return pl.ds(3 * ((step + 1) // 2), 1)


def slot(step):
    return (step[0] + 1) * 9 + (step[1] + 1) * 3 + (step[2] + 1)


def pieces(x):
    high = x.astype(BF16).astype(F32)
    rest = x - high
    mid = rest.astype(BF16).astype(F32)
    return high, mid, rest - mid


def halves(x):
    high = x.astype(BF16)
    return high, (x - high.astype(F32)).astype(BF16)


def kernel(sizes, off_in, vel_in, mass_in, cnt_in, acc_out, den_out, off, vel, mass, cnt, own, near, u_own, u_near,
           own_q, near_q, near_f, s_b, dens, force, force2, force3, quad, load, send1, recv1, send2, recv2):
    me = tuple(lax.axis_index(a) for a in AXES)
    near_x = 1 - 2 * lax.rem(me[0], 2)
    far_x = -near_x
    plane_dirs = [(0, b, c) for b in SIDES for c in SIDES if (b, c) != (0, 0)]
    near_dirs = [(near_x, b, c) for b in SIDES for c in SIDES]
    far_dirs = [(far_x, b, c) for b in SIDES for c in SIDES]
    all_dirs = far_dirs + near_dirs + plane_dirs

    def other(step):
        return tuple(m + s for m, s in zip(me, step))

    def exists(step):
        ok = None
        for m, s, n in zip(me, step, sizes):
            if isinstance(s, int) and s == 0:
                continue
            here = jnp.logical_and(m + s >= 0, m + s < n)
            ok = here if ok is None else jnp.logical_and(ok, here)
        return ok

    def neg(step):
        return tuple(-s for s in step)

    loads = [
        pltpu.make_async_copy(src, dst, load.at[k])
        for k, (src, dst) in enumerate(((off_in, off), (mass_in, mass), (cnt_in, cnt), (vel_in, vel)))
    ]
    for item in loads:
        item.start()
    barrier = pltpu.get_barrier_semaphore()
    for step in all_dirs:
        @pl.when(exists(step))
        def _():
            pl.semaphore_signal(barrier, inc=1, device_id=other(step), device_id_type=MESH)
    for item in loads:
        item.wait()

    lanes = lax.broadcasted_iota(jnp.int32, (1, 128), 1)
    one = jnp.ones((1, 128), F32)
    blank = jnp.zeros((3, 128), F32)

    def put_near_q(a, b, c, scaled, rest):
        high, mid, low = pieces(jnp.concatenate(scaled + [rest, one, blank], axis=0))
        near_q[a, b, c] = jnp.concatenate([high, mid, high, mid, low, high], axis=0).astype(BF16)

    def own_tile(x, y, z):
        pos = [off[k, x, y, z : z + 1, :] + float(c - 1) for k, c in enumerate((x, y, z))]
        m_eff = jnp.where(lanes < cnt[x, y, z], mass[x, y, z : z + 1, :], 0.0)
        sq = pos[0] * pos[0] + pos[1] * pos[1] + pos[2] * pos[2]
        v = [vel[k, x, y, z : z + 1, :] for k in range(3)]
        return pos, m_eff, v, sq

    for x in range(2):
        for y in range(2):
            for z in range(2):
                pos, m_eff, v, sq = own_tile(x, y, z)
                own[x, y, z] = jnp.concatenate(pos + [m_eff] + v + [sq], axis=0)

    peers = 1
    for m, n in zip(me, sizes):
        peers = peers * (1 + (m > 0).astype(jnp.int32) + (m < n - 1).astype(jnp.int32))
    pl.semaphore_wait(barrier, peers - 1)

    def copy1(step, incoming):
        there = step if incoming else neg(step)
        return pltpu.make_async_remote_copy(
            src_ref=own.at[tuple(span_own(s) for s in step)],
            dst_ref=near.at[tuple(span_halo(s) for s in there)],
            send_sem=send1.at[slot(step)],
            recv_sem=recv1.at[slot(there)],
            device_id=other(step),
            device_id_type=MESH,
        )

    def copy2(step, incoming):
        there = step if incoming else neg(step)
        return pltpu.make_async_remote_copy(
            src_ref=u_own.at[tuple(span_own(s) for s in step)],
            dst_ref=u_near.at[tuple(span_halo(s) for s in there)],
            send_sem=send2.at[slot(step)],
            recv_sem=recv2.at[slot(there)],
            device_id=other(step),
            device_id_type=MESH,
        )

    for step in all_dirs:
        @pl.when(exists(step))
        def _():
            copy1(step, False).start()

    for x in range(2):
        for y in range(2):
            for z in range(2):
                pos, m_eff, v, sq = own_tile(x, y, z)
                scaled = [p * -6.0 for p in pos]
                near[1 + x, 1 + y, 1 + z] = jnp.concatenate(scaled + [m_eff] + v + [jnp.zeros_like(sq)], axis=0)
                put_near_q(1 + x, 1 + y, 1 + z, scaled, 1.0 - sq)
                high, mid, low = pieces(jnp.concatenate([p * (-1.0 / 3.0) for p in pos] + [one, -sq, blank], axis=0))
                stack = jnp.concatenate([high, high, mid, mid, high, low], axis=0)
                own_q[4 * x + 2 * y + z] = jnp.transpose(stack, (1, 0)).astype(BF16)

    def cells_own(x, y, z):
        return [(a, b, c) for a in (1, 2) for b in (1, 2) for c in (1, 2)]

    def cells_plane(x, y, z):
        bh, ch = 3 * y, 3 * z
        shared = [(a, bh, c) for a in (1, 2) for c in (1, 2)]
        return shared + [(a, b, ch) for a in (1, 2) for b in (bh, 1, 2)]

    def cells_side(x, y, z):
        shared = [(3 * x, y + b, c) for b in range(3) for c in (1, 2)]
        return shared + [(3 * x, y + b, 3 * z) for b in range(3)]

    def density_cells(x, cells_of, base, first):
        for y in range(2):
            for z in range(2):
                n = 4 * x + 2 * y + z
                cells = cells_of(x, y, z)
                mine = own_q[n]
                total = jnp.zeros((128, 128), F32) if first else dens[n]
                for k in range(0, len(cells), 2):
                    group = cells[k : k + 2]
                    them = jnp.concatenate([near_q[cell] for cell in group], axis=1)
                    both = jnp.dot(mine, them, preferred_element_type=F32)
                    for i, (a, b, c) in enumerate(group):
                        q = jnp.maximum(both[:, 128 * i : 128 * i + 128], 0.0)
                        quad[n, base + k + i] = q
                        total = total + (q * q) * (q * near[a, b, c, 3:4, :])
                dens[n] = total

    def force_pair(x, y, cells_of, base, shared, first):
        n = 4 * x + 2 * y
        pair = 2 * x + y
        rows2 = jnp.zeros((32, 256), F32) if first else force2[pair]
        rows3 = jnp.zeros((16, 256), F32) if first else force3[pair]
        cells = cells_of(x, y, 0)
        for k in range(0, shared, 2):
            f = jnp.concatenate([near_f[cells[k]], near_f[cells[k + 1]]], axis=1)
            q = jnp.concatenate(
                [jnp.concatenate([quad[n + z, base + k + i] for i in range(2)], axis=1) for z in range(2)], axis=0
            )
            q2 = q * q
            for part in halves(q2):
                rows2 = rows2 + lax.dot_general(f[:32], part, LAST, preferred_element_type=F32)
            for part in halves(q2 * q):
                rows3 = rows3 + lax.dot_general(f[32:], part, LAST, preferred_element_type=F32)
        force2[pair] = rows2
        force3[pair] = rows3
        for z in range(2):
            rest = list(enumerate(cells_of(x, y, z)))[shared:]
            for r0 in range(0, 128, TILE):
                rows = pl.ds(r0, TILE)
                si = s_b[n + z, rows, :]
                sums = [jnp.zeros((TILE, 128), F32) if first else force[k, n + z, rows, :] for k in range(5)]
                for k, (a, b, c) in rest:
                    t = near[a, b, c]
                    q = quad[n + z, base + k, rows, :]
                    q2 = q * q
                    pr = q2 * (t[3:4] * si + t[7:8])
                    vi = q2 * (q * t[7:8])
                    for d in range(3):
                        sums[d] = sums[d] + (pr * t[d : d + 1] + vi * t[4 + d : 5 + d])
                    sums[3] = sums[3] + pr
                    sums[4] = sums[4] + vi
                for k in range(5):
                    force[k, n + z, rows, :] = sums[k]

    def over_x(fn):
        def step(x, carry):
            fn(x)
            return carry

        lax.fori_loop(0, 2, step, 0)

    def force_cells(x, cells_of, base, shared, first):
        for y in range(2):
            force_pair(x, y, cells_of, base, shared, first)

    def corner(step):
        def low(s):
            return 1 if isinstance(s, int) and s == 0 else 3 * ((s + 1) // 2)

        def many(s):
            return 2 if isinstance(s, int) and s == 0 else 1

        return [
            tuple(low(s) + i for s, i in zip(step, (i, j, k)))
            for i in range(many(step[0]))
            for j in range(many(step[1]))
            for k in range(many(step[2]))
        ]

    def arrive1(dirs):
        for step in dirs:
            cells = corner(step)

            @pl.when(exists(step))
            def _():
                copy1(step, True).wait_recv()
                for a, b, c in cells:
                    t = near[a, b, c]
                    pos = []
                    for k in range(3):
                        shift = 2 * step[k]
                        pos.append(t[k : k + 1] + (float(shift) if isinstance(shift, int) else shift.astype(F32)))
                    sq = pos[0] * pos[0] + pos[1] * pos[1] + pos[2] * pos[2]
                    scaled = [p * -6.0 for p in pos]
                    near[a, b, c, 0:3, :] = jnp.concatenate(scaled, axis=0)
                    put_near_q(a, b, c, scaled, 1.0 - sq)

            @pl.when(jnp.logical_not(exists(step)))
            def _():
                for cell in cells:
                    near[cell] = jnp.zeros((8, 128), F32)
                    near_q[cell] = jnp.zeros((48, 128), BF16)

    def put_near_f(a, b, c, u):
        t = near[a, b, c]
        m = t[3:4]
        wide = jnp.concatenate([m] + [m * t[k : k + 1] for k in range(3)] + [u] + [u * t[k : k + 1] for k in range(3)], axis=0)
        thin = jnp.concatenate([u] + [u * t[4 + k : 5 + k] for k in range(3)], axis=0)
        wide3, thin3 = pieces(wide), pieces(thin)
        near_f[a, b, c] = jnp.concatenate(
            list(wide3) + [jnp.zeros_like(wide)] + list(thin3) + [jnp.zeros_like(thin)], axis=0
        ).astype(BF16)

    def arrive2(dirs):
        for step in dirs:
            cells = corner(step)
            inner = isinstance(step[2], int) and step[2] == 0

            @pl.when(exists(step))
            def _():
                copy2(step, True).wait_recv()
                for a, b, c in cells:
                    u = u_near[a, b, c]
                    near[a, b, c, 7:8, :] = u
                    if inner:
                        put_near_f(a, b, c, u)

            if inner:
                @pl.when(jnp.logical_not(exists(step)))
                def _():
                    for cell in cells:
                        near_f[cell] = jnp.zeros((48, 128), BF16)

    near_side, far_side = (near_x + 1) // 2, (far_x + 1) // 2
    over_x(lambda x: density_cells(x, cells_own, 0, True))
    arrive1(plane_dirs)
    over_x(lambda x: density_cells(x, cells_plane, 8, False))
    arrive1(near_dirs)
    density_cells(near_side, cells_side, 18, False)
    arrive1(far_dirs)
    density_cells(far_side, cells_side, 18, False)

    s_rows = []
    for n in range(8):
        x, y, z = n // 4, (n // 2) % 2, n % 2
        rho = KERNEL_NORM * jnp.sum(jnp.transpose(dens[n], (1, 0)), axis=0, keepdims=True)
        held = lanes < cnt[x, y, z]
        rho = jnp.where(held, rho, 0.0)
        den_out[x, y, z : z + 1, :] = rho
        s = PRESSURE_COEF / jnp.where(held, rho, 1.0)
        s_rows.append(s)
        u = own[x, y, z, 3:4, :] * s
        u_own[x, y, z] = u

    for step in all_dirs:
        @pl.when(exists(step))
        def _():
            copy2(step, False).start()

    s_all = jnp.concatenate(s_rows, axis=0)
    turned = jnp.transpose(s_all, (1, 0))
    for n in range(8):
        x, y, z = n // 4, (n // 2) % 2, n % 2
        s_b[n] = jnp.broadcast_to(turned[:, n : n + 1], (128, 128))
        u = own[x, y, z, 3:4, :] * s_rows[n]
        near[1 + x, 1 + y, 1 + z, 7:8, :] = u
        put_near_f(1 + x, 1 + y, 1 + z, u)

    over_x(lambda x: force_cells(x, cells_own, 0, SHARED[0], True))
    arrive2(plane_dirs)
    over_x(lambda x: force_cells(x, cells_plane, 8, SHARED[1], False))
    arrive2(near_dirs)
    force_cells(near_side, cells_side, 18, SHARED[2], False)
    arrive2(far_dirs)
    force_cells(far_side, cells_side, 18, SHARED[2], False)

    for n in range(8):
        x, y, z = n // 4, (n // 2) % 2, n % 2
        f = [jnp.sum(jnp.transpose(force[k, n], (1, 0)), axis=0, keepdims=True) for k in range(5)]
        g = force2[2 * x + y, :, 128 * z : 128 * z + 128]
        g = g[0:8] + g[8:16] + g[16:24]
        h = force3[2 * x + y, :, 128 * z : 128 * z + 128]
        h = h[0:4] + h[4:8] + h[8:12]
        held = lanes < cnt[x, y, z]
        t = own[x, y, z]
        s = s_rows[n]
        press = f[3] + s * g[0:1] + g[4:5]
        drag = f[4] + h[0:1]
        for k in range(3):
            a = f[k] + s * g[1 + k : 2 + k] + g[5 + k : 6 + k] + h[1 + k : 2 + k]
            a = KERNEL_NORM * (a + GRADIENT_RATIO * t[k : k + 1] * press - t[4 + k : 5 + k] * drag)
            acc_out[k, x, y, z : z + 1, :] = jnp.where(held, a, 0.0)

    for step in all_dirs:
        @pl.when(exists(step))
        def _():
            copy1(step, False).wait_send()
            copy2(step, False).wait_send()


def local(sizes, offsets, velocity, mass, counts):
    vmem = pl.BlockSpec(memory_space=pltpu.VMEM)
    hbm = pl.BlockSpec(memory_space=pltpu.HBM)
    return pl.pallas_call(
        functools.partial(kernel, sizes),
        out_shape=(
            jax.ShapeDtypeStruct(offsets.shape, F32),
            jax.ShapeDtypeStruct(mass.shape, F32),
        ),
        in_specs=[hbm, hbm, hbm, hbm],
        out_specs=(vmem, vmem),
        scratch_shapes=[
            pltpu.VMEM(offsets.shape, F32),
            pltpu.VMEM(velocity.shape, F32),
            pltpu.VMEM(mass.shape, F32),
            pltpu.SMEM(counts.shape, jnp.int32),
            pltpu.VMEM((2, 2, 2, 8, 128), F32),
            pltpu.VMEM((4, 4, 4, 8, 128), F32),
            pltpu.VMEM((2, 2, 2, 1, 128), F32),
            pltpu.VMEM((4, 4, 4, 1, 128), F32),
            pltpu.VMEM((8, 128, 48), BF16),
            pltpu.VMEM((4, 4, 4, 48, 128), BF16),
            pltpu.VMEM((4, 4, 4, 48, 128), BF16),
            pltpu.VMEM((8, 128, 128), F32),
            pltpu.VMEM((8, 128, 128), F32),
            pltpu.VMEM((5, 8, 128, 128), F32),
            pltpu.VMEM((4, 32, 256), F32),
            pltpu.VMEM((4, 16, 256), F32),
            pltpu.VMEM((8, 27, 128, 128), F32),
            pltpu.SemaphoreType.DMA((4,)),
            pltpu.SemaphoreType.DMA((27,)),
            pltpu.SemaphoreType.DMA((27,)),
            pltpu.SemaphoreType.DMA((27,)),
            pltpu.SemaphoreType.DMA((27,)),
        ],
        compiler_params=pltpu.CompilerParams(
            collective_id=0, has_side_effects=True, vmem_limit_bytes=56 * 2**20
        ),
        name="sph",
    )(offsets, velocity, mass, counts)


def solution(mesh):
    sizes = tuple(mesh.shape[a] for a in AXES)
    in_specs = (
        P(None, "gx", "gy", "gz", None),
        P(None, "gx", "gy", "gz", None),
        P("gx", "gy", "gz", None),
        P("gx", "gy", "gz"),
    )
    out_specs = (P(None, "gx", "gy", "gz", None), P("gx", "gy", "gz", None))
    return jax.shard_map(
        functools.partial(local, sizes), mesh=mesh, in_specs=in_specs, out_specs=out_specs, check_vma=False
    )
```

```python
import functools
import math

import jax
import jax.numpy as jnp
from jax import lax
from jax.experimental import pallas as pl
from jax.experimental.pallas import tpu as pltpu
from jax.sharding import PartitionSpec as P

KERNEL_NORM = 315.0 / (64.0 * math.pi)
GRADIENT_RATIO = 6.0
PRESSURE_COEF = 0.5
AXES = ("gx", "gy", "gz")
SIDES = (-1, 0, 1)
MESH = pl.DeviceIdType.MESH
F32 = jnp.float32
BF16 = jnp.bfloat16
TILE = 32
LAST = (((1,), (1,)), ((), ()))
SHARED = (4, 4, 4, 2)
WHOLE = (8, 10, 6, 3)
SHARED_BASE = tuple(sum(SHARED[:k]) for k in range(5))
REST_BASE = tuple(sum(WHOLE[:k]) - sum(SHARED[:k]) for k in range(5))


def span_own(step):
    if isinstance(step, int):
        return pl.ds(0, 2) if step == 0 else pl.ds((step + 1) // 2, 1)
    return pl.ds((step + 1) // 2, 1)


def span_halo(step):
    if isinstance(step, int):
        return pl.ds(1, 2) if step == 0 else pl.ds(0 if step < 0 else 3, 1)
    return pl.ds(3 * ((step + 1) // 2), 1)


def slot(step):
    return (step[0] + 1) * 9 + (step[1] + 1) * 3 + (step[2] + 1)


def pieces(x):
    high = x.astype(BF16).astype(F32)
    rest = x - high
    mid = rest.astype(BF16).astype(F32)
    return high, mid, rest - mid


def halves(x):
    high = x.astype(BF16)
    return high, (x - high.astype(F32)).astype(BF16)


def kernel(sizes, off_in, vel_in, mass_in, cnt_in, acc_out, den_out, off, vel, mass, cnt, own, near, s_own, u_own, u_near,
           own_q, near_q, near_f, s_b, dens, force, force2, force3, quad, split, load, send1, recv1, send2, recv2):
    me = tuple(lax.axis_index(a) for a in AXES)
    near_x = 1 - 2 * lax.rem(me[0], 2)
    far_x = -near_x
    plane_dirs = [(0, b, c) for b in SIDES for c in SIDES if (b, c) != (0, 0)]
    near_dirs = [(near_x, b, c) for b in SIDES for c in SIDES]
    far_dirs = [(far_x, b, c) for b in SIDES for c in SIDES]
    all_dirs = far_dirs + near_dirs + plane_dirs

    def other(step):
        return tuple(m + s for m, s in zip(me, step))

    def exists(step):
        ok = None
        for m, s, n in zip(me, step, sizes):
            if isinstance(s, int) and s == 0:
                continue
            here = jnp.logical_and(m + s >= 0, m + s < n)
            ok = here if ok is None else jnp.logical_and(ok, here)
        return ok

    def neg(step):
        return tuple(-s for s in step)

    loads = [
        pltpu.make_async_copy(src, dst, load.at[k])
        for k, (src, dst) in enumerate(((off_in, off), (mass_in, mass), (cnt_in, cnt), (vel_in, vel)))
    ]
    for item in loads:
        item.start()
    barrier = pltpu.get_barrier_semaphore()
    for step in all_dirs:
        @pl.when(exists(step))
        def _():
            pl.semaphore_signal(barrier, inc=1, device_id=other(step), device_id_type=MESH)
    for item in loads:
        item.wait()

    lanes = lax.broadcasted_iota(jnp.int32, (1, 128), 1)
    one = jnp.ones((1, 128), F32)
    blank = jnp.zeros((3, 128), F32)

    def put_near_q(a, b, c, scaled, rest):
        high, mid, low = pieces(jnp.concatenate(scaled + [rest, one, blank], axis=0))
        near_q[a, b, c] = jnp.concatenate([high, mid, high, mid, low, high], axis=0).astype(BF16)

    def own_tile(x, y, z):
        pos = [off[k, x, y, z : z + 1, :] + float(c - 1) for k, c in enumerate((x, y, z))]
        m_eff = jnp.where(lanes < cnt[x, y, z], mass[x, y, z : z + 1, :], 0.0)
        sq = pos[0] * pos[0] + pos[1] * pos[1] + pos[2] * pos[2]
        v = [vel[k, x, y, z : z + 1, :] for k in range(3)]
        return pos, m_eff, v, sq

    for x in range(2):
        for y in range(2):
            for z in range(2):
                pos, m_eff, v, sq = own_tile(x, y, z)
                own[x, y, z] = jnp.concatenate(pos + [m_eff] + v + [sq], axis=0)

    peers = 1
    for m, n in zip(me, sizes):
        peers = peers * (1 + (m > 0).astype(jnp.int32) + (m < n - 1).astype(jnp.int32))
    pl.semaphore_wait(barrier, peers - 1)

    def copy1(step, incoming):
        there = step if incoming else neg(step)
        return pltpu.make_async_remote_copy(
            src_ref=own.at[tuple(span_own(s) for s in step)],
            dst_ref=near.at[tuple(span_halo(s) for s in there)],
            send_sem=send1.at[slot(step)],
            recv_sem=recv1.at[slot(there)],
            device_id=other(step),
            device_id_type=MESH,
        )

    def copy2(step, incoming):
        there = step if incoming else neg(step)
        return pltpu.make_async_remote_copy(
            src_ref=u_own.at[tuple(span_own(s) for s in step)],
            dst_ref=u_near.at[tuple(span_halo(s) for s in there)],
            send_sem=send2.at[slot(step)],
            recv_sem=recv2.at[slot(there)],
            device_id=other(step),
            device_id_type=MESH,
        )

    for step in all_dirs:
        @pl.when(exists(step))
        def _():
            copy1(step, False).start()

    for x in range(2):
        for y in range(2):
            for z in range(2):
                pos, m_eff, v, sq = own_tile(x, y, z)
                scaled = [p * -6.0 for p in pos]
                near[1 + x, 1 + y, 1 + z] = jnp.concatenate(scaled + [m_eff] + v + [jnp.zeros_like(sq)], axis=0)
                put_near_q(1 + x, 1 + y, 1 + z, scaled, 1.0 - sq)
                high, mid, low = pieces(jnp.concatenate([p * (-1.0 / 3.0) for p in pos] + [one, -sq, blank], axis=0))
                stack = jnp.concatenate([high, high, mid, mid, high, low], axis=0)
                own_q[4 * x + 2 * y + z] = jnp.transpose(stack, (1, 0)).astype(BF16)

    def cells_own(x, y, z):
        return [(a, b, c) for a in (1, 2) for b in (1, 2) for c in (1, 2)]

    def cells_plane(x, y, z):
        bh, ch = 3 * y, 3 * z
        shared = [(a, bh, c) for a in (1, 2) for c in (1, 2)]
        return shared + [(a, b, ch) for a in (1, 2) for b in (bh, 1, 2)]

    def cells_inner(x, y, z):
        return [(3 * x, b, c) for b in (1, 2) for c in (1, 2)] + [(3 * x, b, 3 * z) for b in (1, 2)]

    def cells_outer(x, y, z):
        return [(3 * x, 3 * y, c) for c in (1, 2, 3 * z)]

    def density_cells(x, cells_of, stage, first):
        shared = SHARED[stage]
        for y in range(2):
            for z in range(2):
                n = 4 * x + 2 * y + z
                cells = cells_of(x, y, z)
                mine = own_q[n]
                total = jnp.zeros((128, 128), F32) if first else dens[n]
                for k in range(0, len(cells), 2):
                    group = cells[k : k + 2]
                    them = jnp.concatenate([near_q[cell] for cell in group], axis=1)
                    both = jnp.dot(mine, them, preferred_element_type=F32)
                    for i, (a, b, c) in enumerate(group):
                        q = jnp.maximum(both[:, 128 * i : 128 * i + 128], 0.0)
                        q2 = q * q
                        q3 = q2 * q
                        if k < shared:
                            place = (n, SHARED_BASE[stage] + k + i)
                            for p, part in enumerate(halves(q2) + halves(q3)):
                                split[(p,) + place] = part
                        else:
                            quad[n, REST_BASE[stage] + k + i - shared] = q
                        total = total + q3 * near[a, b, c, 3:4, :]
                dens[n] = total

    def force_pair(x, y, cells_of, stage, first):
        n = 4 * x + 2 * y
        pair = 2 * x + y
        shared = SHARED[stage]
        cells = cells_of(x, y, 0)
        grams = [
            jnp.zeros((32, 256), F32) if first else force2[pair],
            jnp.zeros((16, 256), F32) if first else force3[pair],
        ]

        def gram(k):
            f = jnp.concatenate([near_f[cells[k]], near_f[cells[k + 1]]], axis=1)
            for p in range(4):
                place = SHARED_BASE[stage] + k
                part = jnp.concatenate(
                    [jnp.concatenate([split[p, n + z, place + i] for i in range(2)], axis=1) for z in range(2)], axis=0
                )
                rows = f[:32] if p < 2 else f[32:]
                grams[p // 2] = grams[p // 2] + lax.dot_general(rows, part, LAST, preferred_element_type=F32)

        def direct(z, r0):
            rest = cells_of(x, y, z)[shared:]
            rows = pl.ds(r0, TILE)
            si = s_b[n + z, rows, :]
            sums = [jnp.zeros((TILE, 128), F32) if first else force[k, n + z, rows, :] for k in range(5)]
            for k, (a, b, c) in enumerate(rest):
                t = near[a, b, c]
                q = quad[n + z, REST_BASE[stage] + k, rows, :]
                q2 = q * q
                pr = q2 * (t[3:4] * si + t[7:8])
                vi = q2 * (q * t[7:8])
                for d in range(3):
                    sums[d] = sums[d] + (pr * t[d : d + 1] + vi * t[4 + d : 5 + d])
                sums[3] = sums[3] + pr
                sums[4] = sums[4] + vi
            for k in range(5):
                force[k, n + z, rows, :] = sums[k]

        tiles = [(z, r0) for z in range(2) for r0 in range(0, 128, TILE)]
        steps = shared // 2
        done = 0
        for k in range(steps):
            gram(2 * k)
            until = len(tiles) * (k + 1) // steps
            for z, r0 in tiles[done:until]:
                direct(z, r0)
            done = until
        for z, r0 in tiles[done:]:
            direct(z, r0)
        force2[pair] = grams[0]
        force3[pair] = grams[1]

    def over_x(fn):
        def step(x, carry):
            fn(x)
            return carry

        lax.fori_loop(0, 2, step, 0)

    def force_cells(x, cells_of, stage, first):
        for y in range(2):
            force_pair(x, y, cells_of, stage, first)

    def corner(step):
        def low(s):
            return 1 if isinstance(s, int) and s == 0 else 3 * ((s + 1) // 2)

        def many(s):
            return 2 if isinstance(s, int) and s == 0 else 1

        return [
            tuple(low(s) + i for s, i in zip(step, (i, j, k)))
            for i in range(many(step[0]))
            for j in range(many(step[1]))
            for k in range(many(step[2]))
        ]

    def arrive1(dirs):
        for step in dirs:
            cells = corner(step)

            @pl.when(exists(step))
            def _():
                copy1(step, True).wait_recv()
                for a, b, c in cells:
                    t = near[a, b, c]
                    pos = []
                    for k in range(3):
                        shift = 2 * step[k]
                        pos.append(t[k : k + 1] + (float(shift) if isinstance(shift, int) else shift.astype(F32)))
                    sq = pos[0] * pos[0] + pos[1] * pos[1] + pos[2] * pos[2]
                    scaled = [p * -6.0 for p in pos]
                    near[a, b, c, 0:3, :] = jnp.concatenate(scaled, axis=0)
                    put_near_q(a, b, c, scaled, 1.0 - sq)

            @pl.when(jnp.logical_not(exists(step)))
            def _():
                for cell in cells:
                    near[cell] = jnp.zeros((8, 128), F32)
                    near_q[cell] = jnp.zeros((48, 128), BF16)

    def put_near_f(a, b, c, u):
        t = near[a, b, c]
        m = t[3:4]
        wide = jnp.concatenate([m] + [m * t[k : k + 1] for k in range(3)] + [u] + [u * t[k : k + 1] for k in range(3)], axis=0)
        thin = jnp.concatenate([u] + [u * t[4 + k : 5 + k] for k in range(3)], axis=0)
        wide3, thin3 = pieces(wide), pieces(thin)
        near_f[a, b, c] = jnp.concatenate(
            list(wide3) + [jnp.zeros_like(wide)] + list(thin3) + [jnp.zeros_like(thin)], axis=0
        ).astype(BF16)

    def arrive2(dirs):
        for step in dirs:
            cells = corner(step)
            inner = isinstance(step[2], int) and step[2] == 0

            @pl.when(exists(step))
            def _():
                copy2(step, True).wait_recv()
                for a, b, c in cells:
                    u = u_near[a, b, c]
                    near[a, b, c, 7:8, :] = u
                    if inner:
                        put_near_f(a, b, c, u)

            if inner:
                @pl.when(jnp.logical_not(exists(step)))
                def _():
                    for cell in cells:
                        near_f[cell] = jnp.zeros((48, 128), BF16)

    def densities(x):
        four = [(y, z) for y in range(2) for z in range(2)]
        rows = []
        for y, z in four:
            rho = KERNEL_NORM * jnp.sum(jnp.transpose(dens[4 * x + 2 * y + z], (1, 0)), axis=0, keepdims=True)
            held = lanes < cnt[x, y, z]
            rho = jnp.where(held, rho, 0.0)
            den_out[x, y, z : z + 1, :] = rho
            s = PRESSURE_COEF / jnp.where(held, rho, 1.0)
            rows.append(s)
            s_own[x, y, z] = s
            u_own[x, y, z] = own[x, y, z, 3:4, :] * s
        return rows

    def prepare(x, rows):
        turned = jnp.transpose(jnp.concatenate(rows + rows, axis=0), (1, 0))
        for k in range(4):
            y, z = k // 2, k % 2
            s_b[4 * x + k] = jnp.broadcast_to(turned[:, k : k + 1], (128, 128))
            u = own[x, y, z, 3:4, :] * rows[k]
            near[1 + x, 1 + y, 1 + z, 7:8, :] = u
            put_near_f(1 + x, 1 + y, 1 + z, u)

    def post2(dirs):
        for step in dirs:
            @pl.when(exists(step))
            def _():
                copy2(step, False).start()

    def finish(x):
        for y in range(2):
            for z in range(2):
                n, pair = 4 * x + 2 * y + z, 2 * x + y
                f = [jnp.sum(jnp.transpose(force[k, n], (1, 0)), axis=0, keepdims=True) for k in range(5)]
                g = force2[pair, :, 128 * z : 128 * z + 128]
                g = g[0:8] + g[8:16] + g[16:24]
                h = force3[pair, :, 128 * z : 128 * z + 128]
                h = h[0:4] + h[4:8] + h[8:12]
                held = lanes < cnt[x, y, z]
                t = own[x, y, z]
                s = s_own[x, y, z]
                press = f[3] + s * g[0:1] + g[4:5]
                drag = f[4] + h[0:1]
                for k in range(3):
                    a = f[k] + s * g[1 + k : 2 + k] + g[5 + k : 6 + k] + h[1 + k : 2 + k]
                    a = KERNEL_NORM * (a + GRADIENT_RATIO * t[k : k + 1] * press - t[4 + k : 5 + k] * drag)
                    acc_out[k, x, y, z : z + 1, :] = jnp.where(held, a, 0.0)

    near_side, far_side = (near_x + 1) // 2, (far_x + 1) // 2
    far_inner, far_outer = [d for d in far_dirs if d[1] == 0], [d for d in far_dirs if d[1] != 0]
    over_x(lambda x: density_cells(x, cells_own, 0, True))
    arrive1(plane_dirs)
    over_x(lambda x: density_cells(x, cells_plane, 1, False))
    arrive1(near_dirs)
    density_cells(near_side, cells_inner, 2, False)
    density_cells(near_side, cells_outer, 3, False)
    rows = densities(near_side)
    post2(near_dirs)
    prepare(near_side, rows)
    arrive1(far_inner)
    density_cells(far_side, cells_inner, 2, False)
    arrive1(far_outer)
    density_cells(far_side, cells_outer, 3, False)
    rows = densities(far_side)
    post2(far_dirs)
    post2(plane_dirs)
    prepare(far_side, rows)

    over_x(lambda x: force_cells(x, cells_own, 0, True))
    arrive2(plane_dirs)
    over_x(lambda x: force_cells(x, cells_plane, 1, False))
    arrive2(near_dirs)
    force_cells(near_side, cells_inner, 2, False)
    force_cells(near_side, cells_outer, 3, False)
    finish(near_side)
    arrive2(far_inner)
    force_cells(far_side, cells_inner, 2, False)
    arrive2(far_outer)
    force_cells(far_side, cells_outer, 3, False)
    finish(far_side)

    for step in all_dirs:
        @pl.when(exists(step))
        def _():
            copy1(step, False).wait_send()
            copy2(step, False).wait_send()


def local(sizes, offsets, velocity, mass, counts):
    vmem = pl.BlockSpec(memory_space=pltpu.VMEM)
    hbm = pl.BlockSpec(memory_space=pltpu.HBM)
    return pl.pallas_call(
        functools.partial(kernel, sizes),
        out_shape=(
            pltpu.VMEM(offsets.shape, F32),
            pltpu.VMEM(mass.shape, F32),
        ),
        in_specs=[hbm, hbm, hbm, hbm],
        out_specs=(vmem, vmem),
        scratch_shapes=[
            pltpu.VMEM(offsets.shape, F32),
            pltpu.VMEM(velocity.shape, F32),
            pltpu.VMEM(mass.shape, F32),
            pltpu.SMEM(counts.shape, jnp.int32),
            pltpu.VMEM((2, 2, 2, 8, 128), F32),
            pltpu.VMEM((4, 4, 4, 8, 128), F32),
            pltpu.VMEM((2, 2, 2, 1, 128), F32),
            pltpu.VMEM((2, 2, 2, 1, 128), F32),
            pltpu.VMEM((4, 4, 4, 1, 128), F32),
            pltpu.VMEM((8, 128, 48), BF16),
            pltpu.VMEM((4, 4, 4, 48, 128), BF16),
            pltpu.VMEM((4, 4, 4, 48, 128), BF16),
            pltpu.VMEM((8, 128, 128), F32),
            pltpu.VMEM((8, 128, 128), F32),
            pltpu.VMEM((5, 8, 128, 128), F32),
            pltpu.VMEM((4, 32, 256), F32),
            pltpu.VMEM((4, 16, 256), F32),
            pltpu.VMEM((8, REST_BASE[4], 128, 128), F32),
            pltpu.VMEM((4, 8, SHARED_BASE[4], 128, 128), BF16),
            pltpu.SemaphoreType.DMA((4,)),
            pltpu.SemaphoreType.DMA((27,)),
            pltpu.SemaphoreType.DMA((27,)),
            pltpu.SemaphoreType.DMA((27,)),
            pltpu.SemaphoreType.DMA((27,)),
        ],
        compiler_params=pltpu.CompilerParams(
            collective_id=0, has_side_effects=True, vmem_limit_bytes=56 * 2**20
        ),
        name="sph",
    )(offsets, velocity, mass, counts)


def solution(mesh):
    sizes = tuple(mesh.shape[a] for a in AXES)
    in_specs = (
        P(None, "gx", "gy", "gz", None),
        P(None, "gx", "gy", "gz", None),
        P("gx", "gy", "gz", None),
        P("gx", "gy", "gz"),
    )
    out_specs = (P(None, "gx", "gy", "gz", None), P("gx", "gy", "gz", None))
    return jax.shard_map(
        functools.partial(local, sizes), mesh=mesh, in_specs=in_specs, out_specs=out_specs, check_vma=False
    )
```

```python
import functools
import math

import jax
import jax.numpy as jnp
from jax import lax
from jax.experimental import pallas as pl
from jax.experimental.pallas import tpu as pltpu
from jax.sharding import PartitionSpec as P

KERNEL_NORM = 315.0 / (64.0 * math.pi)
GRADIENT_RATIO = 6.0
PRESSURE_COEF = 0.5
AXES = ("gx", "gy", "gz")
SIDES = (-1, 0, 1)
MESH = pl.DeviceIdType.MESH
F32 = jnp.float32
BF16 = jnp.bfloat16
TILE = 32
LAST = (((1,), (1,)), ((), ()))
SHARED = (4, 4, 4, 2)
WHOLE = (8, 10, 6, 3)
SHARED_BASE = tuple(sum(SHARED[:k]) for k in range(5))
REST_BASE = tuple(sum(WHOLE[:k]) - sum(SHARED[:k]) for k in range(5))


def span_own(step):
    if isinstance(step, int):
        return pl.ds(0, 2) if step == 0 else pl.ds((step + 1) // 2, 1)
    return pl.ds((step + 1) // 2, 1)


def span_halo(step):
    if isinstance(step, int):
        return pl.ds(1, 2) if step == 0 else pl.ds(0 if step < 0 else 3, 1)
    return pl.ds(3 * ((step + 1) // 2), 1)


def slot(step):
    return (step[0] + 1) * 9 + (step[1] + 1) * 3 + (step[2] + 1)


def pieces(x):
    high = x.astype(BF16).astype(F32)
    rest = x - high
    mid = rest.astype(BF16).astype(F32)
    return high, mid, rest - mid


def halves(x):
    high = x.astype(BF16)
    return high, (x - high.astype(F32)).astype(BF16)


def kernel(sizes, off_in, vel_in, mass_in, cnt_in, acc_out, den_out, off, vel, mass, cnt, own, near, s_own, u_own, u_near,
           own_q, near_q, near_f, s_b, dens, force, force2, force3, quad, split, load, send1, recv1, send2, recv2, send3, recv3):
    me = tuple(lax.axis_index(a) for a in AXES)
    near_x = 1 - 2 * lax.rem(me[0], 2)
    far_x = -near_x
    plane_dirs = [(0, b, c) for b in SIDES for c in SIDES if (b, c) != (0, 0)]
    near_dirs = [(near_x, b, c) for b in SIDES for c in SIDES]
    far_dirs = [(far_x, b, c) for b in SIDES for c in SIDES]
    far_inner, far_outer = [d for d in far_dirs if d[1] == 0], [d for d in far_dirs if d[1] != 0]
    all_dirs = far_outer + far_inner + near_dirs + plane_dirs

    def other(step):
        return tuple(m + s for m, s in zip(me, step))

    def exists(step):
        ok = None
        for m, s, n in zip(me, step, sizes):
            if isinstance(s, int) and s == 0:
                continue
            here = jnp.logical_and(m + s >= 0, m + s < n)
            ok = here if ok is None else jnp.logical_and(ok, here)
        return ok

    def neg(step):
        return tuple(-s for s in step)

    loads = [
        pltpu.make_async_copy(src, dst, load.at[k])
        for k, (src, dst) in enumerate(((off_in, off), (mass_in, mass), (cnt_in, cnt), (vel_in, vel)))
    ]
    barrier = pltpu.get_barrier_semaphore()
    for step in all_dirs:
        @pl.when(exists(step))
        def _():
            pl.semaphore_signal(barrier, inc=1, device_id=other(step), device_id_type=MESH)
    for item in loads:
        item.start()
    for item in loads:
        item.wait()

    lanes = lax.broadcasted_iota(jnp.int32, (1, 128), 1)
    one = jnp.ones((1, 128), F32)
    blank = jnp.zeros((3, 128), F32)

    def put_near_q(a, b, c, scaled, rest):
        high, mid, low = pieces(jnp.concatenate(scaled + [rest, one, blank], axis=0))
        near_q[a, b, c] = jnp.concatenate([high, mid, high, mid, low, high], axis=0).astype(BF16)

    def own_tile(x, y, z):
        pos = [off[k, x, y, z : z + 1, :] + float(c - 1) for k, c in enumerate((x, y, z))]
        m_eff = jnp.where(lanes < cnt[x, y, z], mass[x, y, z : z + 1, :], 0.0)
        sq = pos[0] * pos[0] + pos[1] * pos[1] + pos[2] * pos[2]
        v = [vel[k, x, y, z : z + 1, :] for k in range(3)]
        return pos, m_eff, v, sq

    for x in range(2):
        for y in range(2):
            for z in range(2):
                pos, m_eff, v, sq = own_tile(x, y, z)
                own[x, y, z] = jnp.concatenate(pos + [m_eff] + v + [sq], axis=0)

    peers = 1
    for m, n in zip(me, sizes):
        peers = peers * (1 + (m > 0).astype(jnp.int32) + (m < n - 1).astype(jnp.int32))
    pl.semaphore_wait(barrier, peers - 1)

    def copy1(step, incoming, half=0):
        there = step if incoming else neg(step)
        rows = (pl.ds(4 * half, 4),)
        send, recv = ((send1, recv1), (send3, recv3))[half]
        return pltpu.make_async_remote_copy(
            src_ref=own.at[tuple(span_own(s) for s in step) + rows],
            dst_ref=near.at[tuple(span_halo(s) for s in there) + rows],
            send_sem=send.at[slot(step)],
            recv_sem=recv.at[slot(there)],
            device_id=other(step),
            device_id_type=MESH,
        )

    def copy2(step, incoming):
        there = step if incoming else neg(step)
        return pltpu.make_async_remote_copy(
            src_ref=u_own.at[tuple(span_own(s) for s in step)],
            dst_ref=u_near.at[tuple(span_halo(s) for s in there)],
            send_sem=send2.at[slot(step)],
            recv_sem=recv2.at[slot(there)],
            device_id=other(step),
            device_id_type=MESH,
        )

    for step in all_dirs:
        @pl.when(exists(step))
        def _():
            copy1(step, False).start()

    for step in all_dirs:
        @pl.when(exists(step))
        def _():
            copy1(step, False, 1).start()

    for x in range(2):
        for y in range(2):
            for z in range(2):
                pos, m_eff, v, sq = own_tile(x, y, z)
                scaled = [p * -6.0 for p in pos]
                near[1 + x, 1 + y, 1 + z] = jnp.concatenate(scaled + [m_eff] + v + [jnp.zeros_like(sq)], axis=0)
                put_near_q(1 + x, 1 + y, 1 + z, scaled, 1.0 - sq)
                high, mid, low = pieces(jnp.concatenate([p * (-1.0 / 3.0) for p in pos] + [one, -sq, blank], axis=0))
                stack = jnp.concatenate([high, high, mid, mid, high, low], axis=0)
                own_q[4 * x + 2 * y + z] = jnp.transpose(stack, (1, 0)).astype(BF16)

    def cells_own(x, y, z):
        return [(a, b, c) for a in (1, 2) for b in (1, 2) for c in (1, 2)]

    def cells_plane(x, y, z):
        bh, ch = 3 * y, 3 * z
        shared = [(a, bh, c) for a in (1, 2) for c in (1, 2)]
        return shared + [(a, b, ch) for a in (1, 2) for b in (bh, 1, 2)]

    def cells_inner(x, y, z):
        return [(3 * x, b, c) for b in (1, 2) for c in (1, 2)] + [(3 * x, b, 3 * z) for b in (1, 2)]

    def cells_outer(x, y, z):
        return [(3 * x, 3 * y, c) for c in (1, 2, 3 * z)]

    def density_cells(x, cells_of, stage, first):
        shared = SHARED[stage]
        for y in range(2):
            for z in range(2):
                n = 4 * x + 2 * y + z
                cells = cells_of(x, y, z)
                mine = own_q[n]
                total = jnp.zeros((128, 128), F32) if first else dens[n]
                for k in range(0, len(cells), 2):
                    group = cells[k : k + 2]
                    them = jnp.concatenate([near_q[cell] for cell in group], axis=1)
                    both = jnp.dot(mine, them, preferred_element_type=F32)
                    for i, (a, b, c) in enumerate(group):
                        q = jnp.maximum(both[:, 128 * i : 128 * i + 128], 0.0)
                        q2 = q * q
                        q3 = q2 * q
                        if k < shared:
                            place = (n, SHARED_BASE[stage] + k + i)
                            for p, part in enumerate(halves(q2) + halves(q3)):
                                split[(p,) + place] = part
                        else:
                            quad[n, REST_BASE[stage] + k + i - shared] = q
                        total = total + q3 * near[a, b, c, 3:4, :]
                dens[n] = total

    def force_pair(x, y, cells_of, stage, first):
        n = 4 * x + 2 * y
        pair = 2 * x + y
        shared = SHARED[stage]
        cells = cells_of(x, y, 0)
        grams = [
            jnp.zeros((32, 256), F32) if first else force2[pair],
            jnp.zeros((16, 256), F32) if first else force3[pair],
        ]

        def gram(k):
            f = jnp.concatenate([near_f[cells[k]], near_f[cells[k + 1]]], axis=1)
            for p in range(4):
                place = SHARED_BASE[stage] + k
                part = jnp.concatenate(
                    [jnp.concatenate([split[p, n + z, place + i] for i in range(2)], axis=1) for z in range(2)], axis=0
                )
                rows = f[:32] if p < 2 else f[32:]
                grams[p // 2] = grams[p // 2] + lax.dot_general(rows, part, LAST, preferred_element_type=F32)

        def direct(z, r0):
            rest = cells_of(x, y, z)[shared:]
            rows = pl.ds(r0, TILE)
            si = s_b[n + z, rows, :]
            sums = [jnp.zeros((TILE, 128), F32) if first else force[k, n + z, rows, :] for k in range(5)]
            for k, (a, b, c) in enumerate(rest):
                t = near[a, b, c]
                q = quad[n + z, REST_BASE[stage] + k, rows, :]
                q2 = q * q
                pr = q2 * (t[3:4] * si + t[7:8])
                vi = q2 * (q * t[7:8])
                for d in range(3):
                    sums[d] = sums[d] + (pr * t[d : d + 1] + vi * t[4 + d : 5 + d])
                sums[3] = sums[3] + pr
                sums[4] = sums[4] + vi
            for k in range(5):
                force[k, n + z, rows, :] = sums[k]

        tiles = [(z, r0) for z in range(2) for r0 in range(0, 128, TILE)]
        steps = shared // 2
        done = 0
        for k in range(steps):
            gram(2 * k)
            until = len(tiles) * (k + 1) // steps
            for z, r0 in tiles[done:until]:
                direct(z, r0)
            done = until
        for z, r0 in tiles[done:]:
            direct(z, r0)
        force2[pair] = grams[0]
        force3[pair] = grams[1]

    def over_x(fn):
        def step(x, carry):
            fn(x)
            return carry

        lax.fori_loop(0, 2, step, 0)

    def force_cells(x, cells_of, stage, first):
        for y in range(2):
            force_pair(x, y, cells_of, stage, first)

    def corner(step):
        def low(s):
            return 1 if isinstance(s, int) and s == 0 else 3 * ((s + 1) // 2)

        def many(s):
            return 2 if isinstance(s, int) and s == 0 else 1

        return [
            tuple(low(s) + i for s, i in zip(step, (i, j, k)))
            for i in range(many(step[0]))
            for j in range(many(step[1]))
            for k in range(many(step[2]))
        ]

    def clear(dirs):
        for step in dirs:
            @pl.when(jnp.logical_not(exists(step)))
            def _():
                for cell in corner(step):
                    near[cell] = jnp.zeros((8, 128), F32)
                    u_near[cell] = jnp.zeros((1, 128), F32)

    def arrive1(dirs):
        for step in dirs:
            @pl.when(exists(step))
            def _():
                copy1(step, True).wait_recv()

        for step in dirs:
            for a, b, c in corner(step):
                t = near[a, b, c, 0:4, :]
                pos = []
                for k in range(3):
                    shift = 2 * step[k]
                    pos.append(t[k : k + 1] + (float(shift) if isinstance(shift, int) else shift.astype(F32)))
                sq = pos[0] * pos[0] + pos[1] * pos[1] + pos[2] * pos[2]
                scaled = [p * -6.0 for p in pos]
                near[a, b, c, 0:3, :] = jnp.concatenate(scaled, axis=0)
                put_near_q(a, b, c, scaled, 1.0 - sq)

    def put_near_f(a, b, c, u):
        t = near[a, b, c]
        m = t[3:4]
        wide = jnp.concatenate([m] + [m * t[k : k + 1] for k in range(3)] + [u] + [u * t[k : k + 1] for k in range(3)], axis=0)
        thin = jnp.concatenate([u] + [u * t[4 + k : 5 + k] for k in range(3)], axis=0)
        wide3, thin3 = pieces(wide), pieces(thin)
        near_f[a, b, c] = jnp.concatenate(
            list(wide3) + [jnp.zeros_like(wide)] + list(thin3) + [jnp.zeros_like(thin)], axis=0
        ).astype(BF16)

    def arrive2(dirs):
        for step in dirs:
            @pl.when(exists(step))
            def _():
                copy1(step, True, 1).wait_recv()
                copy2(step, True).wait_recv()

        for step in dirs:
            inner = isinstance(step[2], int) and step[2] == 0
            for a, b, c in corner(step):
                u = u_near[a, b, c]
                near[a, b, c, 7:8, :] = u
                if inner:
                    put_near_f(a, b, c, u)

    def densities(x):
        four = [(y, z) for y in range(2) for z in range(2)]
        rows = []
        for y, z in four:
            rho = KERNEL_NORM * jnp.sum(jnp.transpose(dens[4 * x + 2 * y + z], (1, 0)), axis=0, keepdims=True)
            held = lanes < cnt[x, y, z]
            rho = jnp.where(held, rho, 0.0)
            den_out[x, y, z : z + 1, :] = rho
            s = PRESSURE_COEF / jnp.where(held, rho, 1.0)
            rows.append(s)
            s_own[x, y, z] = s
            u_own[x, y, z] = own[x, y, z, 3:4, :] * s
        return rows

    def prepare(x, rows):
        turned = jnp.transpose(jnp.concatenate(rows + rows, axis=0), (1, 0))
        for k in range(4):
            y, z = k // 2, k % 2
            s_b[4 * x + k] = jnp.broadcast_to(turned[:, k : k + 1], (128, 128))
            u = own[x, y, z, 3:4, :] * rows[k]
            near[1 + x, 1 + y, 1 + z, 7:8, :] = u
            put_near_f(1 + x, 1 + y, 1 + z, u)

    def post2(dirs):
        for step in dirs:
            @pl.when(exists(step))
            def _():
                copy2(step, False).start()

    def finish(x):
        for y in range(2):
            for z in range(2):
                n, pair = 4 * x + 2 * y + z, 2 * x + y
                f = [jnp.sum(jnp.transpose(force[k, n], (1, 0)), axis=0, keepdims=True) for k in range(5)]
                g = force2[pair, :, 128 * z : 128 * z + 128]
                g = g[0:8] + g[8:16] + g[16:24]
                h = force3[pair, :, 128 * z : 128 * z + 128]
                h = h[0:4] + h[4:8] + h[8:12]
                held = lanes < cnt[x, y, z]
                t = own[x, y, z]
                s = s_own[x, y, z]
                press = f[3] + s * g[0:1] + g[4:5]
                drag = f[4] + h[0:1]
                for k in range(3):
                    a = f[k] + s * g[1 + k : 2 + k] + g[5 + k : 6 + k] + h[1 + k : 2 + k]
                    a = KERNEL_NORM * (a + GRADIENT_RATIO * t[k : k + 1] * press - t[4 + k : 5 + k] * drag)
                    acc_out[k, x, y, z : z + 1, :] = jnp.where(held, a, 0.0)

    near_side, far_side = (near_x + 1) // 2, (far_x + 1) // 2
    clear(all_dirs)
    over_x(lambda x: density_cells(x, cells_own, 0, True))
    arrive1(plane_dirs)
    over_x(lambda x: density_cells(x, cells_plane, 1, False))
    arrive1(near_dirs)
    density_cells(near_side, cells_inner, 2, False)
    density_cells(near_side, cells_outer, 3, False)
    rows = densities(near_side)
    post2(near_dirs)
    prepare(near_side, rows)
    arrive1(far_inner)
    density_cells(far_side, cells_inner, 2, False)
    arrive1(far_outer)
    density_cells(far_side, cells_outer, 3, False)
    rows = densities(far_side)
    post2(far_outer)
    post2(far_inner)
    post2(plane_dirs)
    prepare(far_side, rows)

    over_x(lambda x: force_cells(x, cells_own, 0, True))
    arrive2(plane_dirs)
    over_x(lambda x: force_cells(x, cells_plane, 1, False))
    arrive2(near_dirs)
    force_cells(near_side, cells_inner, 2, False)
    force_cells(near_side, cells_outer, 3, False)
    finish(near_side)
    arrive2(far_inner)
    force_cells(far_side, cells_inner, 2, False)
    arrive2(far_outer)
    force_cells(far_side, cells_outer, 3, False)
    finish(far_side)

    for step in all_dirs:
        @pl.when(exists(step))
        def _():
            copy1(step, False).wait_send()
            copy1(step, False, 1).wait_send()
            copy2(step, False).wait_send()


def local(sizes, offsets, velocity, mass, counts):
    vmem = pl.BlockSpec(memory_space=pltpu.VMEM)
    hbm = pl.BlockSpec(memory_space=pltpu.HBM)
    return pl.pallas_call(
        functools.partial(kernel, sizes),
        out_shape=(
            pltpu.VMEM(offsets.shape, F32),
            pltpu.VMEM(mass.shape, F32),
        ),
        in_specs=[hbm, hbm, hbm, hbm],
        out_specs=(vmem, vmem),
        scratch_shapes=[
            pltpu.VMEM(offsets.shape, F32),
            pltpu.VMEM(velocity.shape, F32),
            pltpu.VMEM(mass.shape, F32),
            pltpu.SMEM(counts.shape, jnp.int32),
            pltpu.VMEM((2, 2, 2, 8, 128), F32),
            pltpu.VMEM((4, 4, 4, 8, 128), F32),
            pltpu.VMEM((2, 2, 2, 1, 128), F32),
            pltpu.VMEM((2, 2, 2, 1, 128), F32),
            pltpu.VMEM((4, 4, 4, 1, 128), F32),
            pltpu.VMEM((8, 128, 48), BF16),
            pltpu.VMEM((4, 4, 4, 48, 128), BF16),
            pltpu.VMEM((4, 4, 4, 48, 128), BF16),
            pltpu.VMEM((8, 128, 128), F32),
            pltpu.VMEM((8, 128, 128), F32),
            pltpu.VMEM((5, 8, 128, 128), F32),
            pltpu.VMEM((4, 32, 256), F32),
            pltpu.VMEM((4, 16, 256), F32),
            pltpu.VMEM((8, REST_BASE[4], 128, 128), F32),
            pltpu.VMEM((4, 8, SHARED_BASE[4], 128, 128), BF16),
            pltpu.SemaphoreType.DMA((4,)),
            pltpu.SemaphoreType.DMA((27,)),
            pltpu.SemaphoreType.DMA((27,)),
            pltpu.SemaphoreType.DMA((27,)),
            pltpu.SemaphoreType.DMA((27,)),
            pltpu.SemaphoreType.DMA((27,)),
            pltpu.SemaphoreType.DMA((27,)),
        ],
        compiler_params=pltpu.CompilerParams(
            collective_id=0, has_side_effects=True, vmem_limit_bytes=56 * 2**20
        ),
        name="sph",
    )(offsets, velocity, mass, counts)


def solution(mesh):
    sizes = tuple(mesh.shape[a] for a in AXES)
    in_specs = (
        P(None, "gx", "gy", "gz", None),
        P(None, "gx", "gy", "gz", None),
        P("gx", "gy", "gz", None),
        P("gx", "gy", "gz"),
    )
    out_specs = (P(None, "gx", "gy", "gz", None), P("gx", "gy", "gz", None))
    return jax.shard_map(
        functools.partial(local, sizes), mesh=mesh, in_specs=in_specs, out_specs=out_specs, check_vma=False
    )
```
